256 devices in a mesh: trans: 64 (over x, y, z_hi, core), pw: 4 (over z_lo).
Axes of the slice: x: 4, y: 4, z: 8 (z_hi: 2, z_lo: 4; z = z_hi * 4 + z_lo), core: 2. Of those that a mesh axis runs over, the one named last changes fastest.
Arguments:
- pair_density: bfloat16 [32768, 8192], P('trans', 'pw'), may hold values from -0.3984375 to 0.3984375
- coulomb: float32 [8192], P('pw'), may hold values from 0.1 to 10
- partners: int32 [64, 4], P('trans'), may hold values from 0 to 63, as said below
Outputs:
- kernel_tiles: float32 [256, 512, 512], P('trans', None, 'pw')
The draws below stay inside these ranges and needn't reach their ends.
Inputs may be any that keep to these rules, and one draw needn't show every extreme that they name: partners[i, s] = (i + o) mod 64 for an offset o of 1 to 6; the offsets of one row are distinct.
All inputs are finite; a program needn't handle non-finite values.
Results may differ from the reference program's by a relative error of at most 0.014.
Values may be sent and summed in bfloat16 or wider, within the bound.
No kernel may reach another device: no remote copies, remote signals or barrier semaphores. Data moves between devices by JAX's collectives and lax.ppermute only.
A program may use at most 128 MiB of HBM per device.

```python
import math
import jax
import jax.numpy as jnp
from jax import lax

TB = 512
G = 8192
SLOTS = 4
SPAN = 6
BLOCKS = 64
NT = 32768


def draw_partners(key, part):
    key = jax.random.fold_in(key, 7)
    scores = jax.random.randint(key, (BLOCKS, SPAN), 0, 4096) * SPAN + jnp.arange(SPAN, dtype=jnp.int32)[None, :]
    rows = jnp.arange(BLOCKS, dtype=jnp.int32)
    edge = ((rows == 0) | (rows == BLOCKS - 1))[:, None] & (jnp.arange(SPAN) == SPAN - 1)[None, :]
    scores = scores + edge.astype(jnp.int32) * (4096 * SPAN)
    order = jnp.argsort(-scores, axis=1, stable=True)[:, :SLOTS].astype(jnp.int32)
    return ((rows[:, None] + order + 1) % BLOCKS).astype(jnp.int32)


def level_of(own_key, dims, pieces, low, high):
    def one(position, parts):
        heights = jax.random.uniform(jax.random.fold_in(jax.random.fold_in(own_key, 6), position), (parts,), jnp.float32, low / len(pieces), high / len(pieces))
        return jnp.repeat(jnp.exp(heights), dims[position] // parts).reshape((-1,) + (1,) * (len(dims) - position - 1))

    gain = one(*pieces[0])
    for cut in pieces[1:]:
        gain = gain * one(*cut)
    return gain


def noise(key, extent, spread, limit, cuts=(), held_as=jnp.bfloat16):
    array = jax.random.normal(key, extent, jnp.float32) * spread
    if len(cuts) > 0:
        array = level_of(key, extent, cuts, -0.22, 0.18) * array
    return jnp.clip(array, min=-limit, max=limit).astype(held_as)


def setup_inputs(seed: int = 0) -> dict:
    arg_keys = jax.random.split(jax.random.key(seed), 4)
    return {
        "pair_density": noise(arg_keys[0], (NT, G), 0.05, 0.3984375, ((0, 64), (1, 4))),
        "coulomb": jnp.clip(jnp.exp(math.log(10.0) - 4.6051702 * jax.random.uniform(arg_keys[1], (G,), jnp.float32) ** level_of(arg_keys[1], (G,), ((0, 4),), -0.2, 0.2)), 0.1, 10.0),
        "partners": draw_partners(jax.random.fold_in(arg_keys[3], 71), 0),
    }


def reference(pair_density, coulomb, partners):
    weighted = (pair_density.astype(jnp.float32) * coulomb[None, :]).astype(jnp.bfloat16)

    def owner_tiles(owner):
        own = lax.dynamic_slice_in_dim(weighted, (owner * TB).astype(jnp.int32), TB, 0).astype(jnp.float32)
        row = partners[owner]

        def one(partner):
            other = lax.dynamic_slice_in_dim(pair_density, (partner * TB).astype(jnp.int32), TB, 0).astype(jnp.float32)
            return lax.dot_general(own, other, (((1,), (1,)), ((), ())), preferred_element_type=jnp.float32)

        return lax.map(one, row)

    tiles = lax.map(owner_tiles, jnp.arange(BLOCKS, dtype=jnp.int32))
    return tiles.reshape(BLOCKS * SLOTS, TB, TB)
```

```python
import functools

import jax
import jax.numpy as jnp
from jax import lax
from jax.experimental import pallas as pl
from jax.experimental.pallas import tpu as pltpu
from jax.sharding import PartitionSpec as P

SLOTS = 4
TB = 512
PIECES = 2
AXES = ("trans", "pw")


def place(device):
    trans, pw = divmod(device, 4)
    return trans // 16, trans // 4 % 4, trans // 2 % 2 * 4 + pw, trans % 2


def device_at(x, y, z, core):
    z %= 8
    return (((x % 4 * 4 + y % 4) * 2 + z // 4) * 2 + core) * 4 + z % 4


def send(value, target):
    pairs = []
    for device in range(256):
        there = target(*place(device))
        if there is not None:
            pairs.append((device, device_at(*there)))
    return lax.ppermute(value, AXES, pairs)


def other_half(x, y, z, core):
    return x, y, z + 4, core


def other_core(x, y, z, core):
    return x, y, z, 1 - core


def previous_column(x, y, z, core):
    column = (x * 4 + y - 1) % 16
    return column // 4, column % 4, z, core


def up_one(x, y, z, core):
    return x, y + 1, z, core


def up_to_owner(from_core, x, y, z, core):
    if core != from_core:
        return None
    return (x if y in (3, 0) else x - 1), y + 1, z, 1


def tile_kernel(pieces, table, coulomb, *refs):
    blocks, (out, weighted, held, sems) = refs[:-4], refs[-4:]
    groups = []
    at = 0
    for count in (1, 1, pieces, pieces, 1, 1, pieces, pieces, pieces, pieces):
        groups.append(blocks[at : at + count])
        at += count

    def fetch(number, slot, choices):
        for index in choices:

            @pl.when(number == index)
            def _():
                group = groups[index]
                width = 1024 // len(group)
                for part, ref in enumerate(group):
                    pltpu.make_async_copy(
                        ref, held.at[slot, :, pl.ds(part * width, width)], sems.at[slot]
                    ).start()

    def arrived(slot):
        pltpu.make_async_copy(held.at[slot], held.at[slot], sems.at[slot]).wait()

    fetch(table[0], 0, range(4))
    fetch(table[1], 1, range(4))
    for owner in range(2):
        arrived(owner)
        weighted[owner] = (held[owner].astype(jnp.float32) * coulomb[...]).astype(jnp.bfloat16)
        fetch(table[2 + owner], owner, range(10))

    def step(tile, carry):
        slot = tile % 2
        arrived(slot)
        result = lax.dot_general(
            weighted[tile // SLOTS], held[slot], (((1,), (1,)), ((), ())), preferred_element_type=jnp.float32
        ).astype(jnp.bfloat16)
        for part in range(4):
            out[part, tile] = result[:, part * 128 : (part + 1) * 128]

        @pl.when(tile < 2 * SLOTS - 2)
        def _():
            fetch(table[4 + tile], slot, range(10))

        return carry

    lax.fori_loop(0, 2 * SLOTS, step, 0)


def partial_tiles(table, coulomb, blocks):
    any_spec = pl.BlockSpec(memory_space=pl.ANY)
    return pl.pallas_call(
        functools.partial(tile_kernel, PIECES),
        out_shape=jax.ShapeDtypeStruct((4, 2 * SLOTS, TB, 128), jnp.bfloat16),
        in_specs=[
            pl.BlockSpec(memory_space=pltpu.SMEM),
            pl.BlockSpec(memory_space=pltpu.VMEM),
        ]
        + [any_spec] * len(blocks),
        out_specs=pl.BlockSpec(memory_space=pltpu.VMEM),
        scratch_shapes=[
            pltpu.VMEM((2, TB, 1024), jnp.bfloat16),
            pltpu.VMEM((2, TB, 1024), jnp.bfloat16),
            pltpu.SemaphoreType.DMA((2,)),
        ],
        compiler_params=pltpu.CompilerParams(vmem_limit_bytes=32 * 1024 * 1024),
        cost_estimate=pl.CostEstimate(flops=8 * 2 * TB * TB * 1024, bytes_accessed=12 << 20, transcendentals=0),
    )(table, coulomb, *blocks)


def chain(tiles, owner, way, pw):
    arriving = None
    far = 4 if (way < 0) == (owner == 0) else 3
    for distance in range(far, 0, -1):
        part = lax.dynamic_index_in_dim(tiles, (pw + way * distance) % 4, 0, keepdims=False)
        part = part[owner * SLOTS : (owner + 1) * SLOTS]
        if arriving is not None:
            part = (part.astype(jnp.float32) + arriving.astype(jnp.float32)).astype(jnp.bfloat16)

        def target(x, y, z, core, distance=distance):
            half = (z + way * distance) % 8 // 4
            if core != half:
                return None
            return x, y, z + way, (half if distance > 1 else owner)

        arriving = send(part, target)
    return arriving


def body(pair_density, coulomb, partners):
    mine = lax.axis_index("trans")
    pw = lax.axis_index("pw")
    core = mine % 2
    half = mine // 2 % 2
    width = 1024 // PIECES
    away = [
        lax.dynamic_slice_in_dim(pair_density, (1 - half) * 1024 + i * width, width, 1) for i in range(PIECES)
    ]
    other = [send(piece, other_half) for piece in away]
    keep = lax.dynamic_slice_in_dim(pair_density, half * 1024, 1024, 1)
    keep_next = send(keep, previous_column)
    offsets = (partners - mine) % 64
    both = send(offsets, other_core)
    both = jnp.where(core == 0, jnp.concatenate([offsets, both]), jnp.concatenate([both, offsets]))
    far = send(both, other_half)
    wanted = jnp.where(half == core, both, far)
    keep_swap = send(keep, other_core)
    keep_next_swap = send(keep_next, other_core)
    other_swap, other_next, other_next_swap, last_0, last_1 = [], [], [], [], []
    for i, piece in enumerate(other):
        first = jnp.where(half == 0, keep[:, i * width : (i + 1) * width], piece)
        moved = send(first, up_one)
        follow = send(piece, previous_column)
        other_next.append(follow)
        last_0.append(send(moved, functools.partial(up_to_owner, 0)))
        last_1.append(send(moved, functools.partial(up_to_owner, 1)))
        other_swap.append(send(piece, other_core))
        other_next_swap.append(send(follow, other_core))
    owners = jnp.arange(2, dtype=jnp.int32)
    own_entry = 2 * (core ^ half) + (owners ^ core)
    number = owners[:, None] + wanted + 2 * core
    pair = number // 2
    low = number % 2
    entry = jnp.where(pair < 4, 2 * (pair ^ half) + (low ^ core), 8 + low)
    table = jnp.concatenate([own_entry, entry.reshape(-1)]).astype(jnp.int32)
    weights = lax.dynamic_slice_in_dim(coulomb, half * 1024, 1024, 0).reshape(1, 1024)
    blocks = [keep, keep_swap, *other, *other_swap, keep_next, keep_next_swap, *other_next, *other_next_swap]
    tiles = partial_tiles(table, weights, blocks + last_0 + last_1)
    down_0, up_1 = chain(tiles, 0, -1, pw), chain(tiles, 1, 1, pw)
    down_1, up_0 = chain(tiles, 1, -1, pw), chain(tiles, 0, 1, pw)
    here = lax.dynamic_index_in_dim(tiles, pw, 0, keepdims=False)
    given = send(
        lax.dynamic_slice_in_dim(here, (1 - half) * SLOTS, SLOTS, 0),
        lambda x, y, z, c: (x, y, z, 1 - c) if c == z // 4 else None,
    )
    held = lax.dynamic_slice_in_dim(here, half * SLOTS, SLOTS, 0)
    total = jnp.where(core == half, held, given).astype(jnp.float32)
    total += jnp.where(core == 0, down_0, down_1).astype(jnp.float32)
    return total + jnp.where(core == 0, up_0, up_1).astype(jnp.float32)


def solution(mesh):
    placed = (P("trans", "pw"), P("pw"), P("trans", None))
    return jax.shard_map(
        body, mesh=mesh, in_specs=placed, out_specs=P("trans", None, "pw"), check_vma=False
    )
```

```python
import functools

import jax
import jax.numpy as jnp
from jax import lax
from jax.experimental import pallas as pl
from jax.experimental.pallas import tpu as pltpu
from jax.sharding import PartitionSpec as P

SLOTS = 4
TB = 512
WIDE = 1024
WIDTHS = (640, 384)
DEPTH = 4
AXES = ("trans", "pw")


def place(device):
    trans, pw = divmod(device, 4)
    return trans // 16, trans // 4 % 4, trans // 2 % 2 * 4 + pw, trans % 2


def device_at(x, y, z, core):
    z %= 8
    return (((x % 4 * 4 + y % 4) * 2 + z // 4) * 2 + core) * 4 + z % 4


def send(value, target, half=None):
    pairs = []
    for device in range(256):
        x, y, z, core = place(device)
        there = target(x, y, z, core)
        if there is not None and half in (None, z // 4):
            pairs.append((device, device_at(*there)))
    return lax.ppermute(value, AXES, pairs)


def other_half(x, y, z, core):
    return x, y, z + 4, core


def other_core(x, y, z, core):
    return x, y, z, 1 - core


def to_core_1(x, y, z, core):
    return (x, y, z, 1) if core == 0 else None


def previous_column(x, y, z, core):
    column = (x * 4 + y - 1) % 16
    return column // 4, column % 4, z, core


def two_columns_back(x, y, z, core):
    column = (x * 4 + y - 2) % 16
    return column // 4, column % 4, z, core


def up_one(x, y, z, core):
    return x, y + 1, z, core


def up_to_owner(x, y, z, core):
    return (x if y in (3, 0) else x - 1), y + 1, z, core


def tile_kernel(counts, table, *refs):
    total = sum(counts)
    blocks, outs = refs[:total], refs[total : total + 9]
    weighted, held, weighted_sem, sems = refs[total + 9 :]
    groups = []
    at = 0
    for count in counts:
        groups.append(blocks[at : at + count])
        at += count

    def copies(group, target, sem):
        start = 0
        for ref in group:
            width = ref.shape[1]
            pltpu.make_async_copy(ref.at[pl.ds(0, TB)], target.at[:, pl.ds(start, width)], sem).start()
            start += width

    def whole(target, sem):
        pltpu.make_async_copy(target, target, sem).wait()

    def fetch(tile, slot):
        for index, group in enumerate(groups[2:]):

            @pl.when(table[tile] == index)
            def _():
                copies(group, held.at[slot], sems.at[slot])

    half = table[8]
    z = table[9]
    for which in range(2):

        @pl.when(half == which)
        def _():
            copies(groups[which], weighted.at[0], weighted_sem.at[0])

    fetch(0, 0)
    fetch(1, 1)
    for which in range(2):

        @pl.when(half == which)
        def _():
            copies(groups[1 - which], weighted.at[1], weighted_sem.at[1])

    def step(tile, carry):
        owner = tile // SLOTS
        place = tile % SLOTS
        slot = tile % DEPTH

        @pl.when(tile + 2 < 2 * SLOTS)
        def _():
            fetch(tile + 2, (tile + 2) % DEPTH)

        @pl.when(place == 0)
        def _():
            whole(weighted.at[owner], weighted_sem.at[owner])

        whole(held.at[slot], sems.at[slot])
        result = lax.dot_general(
            weighted[owner], held[slot], (((1,), (1,)), ((), ())), preferred_element_type=jnp.float32
        )
        for part in range(4):
            column = result[:, part * 128 : (part + 1) * 128]
            ahead = (owner * 4 + part - z + 8) % 8

            @pl.when(ahead == 0)
            def _():
                outs[0][place] = column

            for distance in (1, 2, 3, 5, 6, 7):

                @pl.when(ahead == distance)
                def _():
                    outs[distance][place] = column.astype(jnp.bfloat16)

            @pl.when((ahead == 4) & (place < 2))
            def _():
                outs[4][place] = column.astype(jnp.bfloat16)

            @pl.when((ahead == 4) & (place >= 2))
            def _():
                outs[8][place - 2] = column.astype(jnp.bfloat16)

        return carry

    lax.fori_loop(0, 2 * SLOTS, step, 0)


def partial_tiles(table, groups):
    counts = [len(group) for group in groups]
    blocks = [piece for group in groups for piece in group]
    shapes = [jax.ShapeDtypeStruct((SLOTS, TB, 128), jnp.float32)]
    for distance in range(1, 9):
        shapes.append(jax.ShapeDtypeStruct((2 if distance in (4, 8) else SLOTS, TB, 128), jnp.bfloat16))
    return pl.pallas_call(
        functools.partial(tile_kernel, counts),
        out_shape=tuple(shapes),
        in_specs=[pl.BlockSpec(memory_space=pltpu.SMEM)] + [pl.BlockSpec(memory_space=pltpu.HBM)] * len(blocks),
        out_specs=tuple(pl.BlockSpec(memory_space=pltpu.VMEM) for _ in shapes),
        scratch_shapes=[
            pltpu.VMEM((2, TB, WIDE), jnp.bfloat16),
            pltpu.VMEM((DEPTH, TB, WIDE), jnp.bfloat16),
            pltpu.SemaphoreType.DMA((2,)),
            pltpu.SemaphoreType.DMA((DEPTH,)),
        ],
        compiler_params=pltpu.CompilerParams(vmem_limit_bytes=60 * 1024 * 1024),
        cost_estimate=pl.CostEstimate(flops=8 * 2 * TB * TB * WIDE, bytes_accessed=15 << 20, transcendentals=0),
    )(table, *blocks)


def together(*values):
    return lax.optimization_barrier(values)


def ring(parts):
    def ahead(x, y, z, core):
        return x, y, z + 1, core

    def behind(x, y, z, core):
        return x, y, z - 1, core

    down, up = together(send(parts[4], behind), send(parts[8], ahead))
    for distance in range(3, 0, -1):
        lower, upper = parts[8 - distance].astype(jnp.float32), parts[distance].astype(jnp.float32)
        if distance == 3:
            down = jnp.concatenate([down, jnp.zeros_like(down)])
            up = jnp.concatenate([jnp.zeros_like(up), up])
        down = (lower + down.astype(jnp.float32)).astype(jnp.bfloat16)
        up = (upper + up.astype(jnp.float32)).astype(jnp.bfloat16)
        down, up = together(down, up)
        down, up = together(send(down, behind), send(up, ahead))
    return parts[0] + down.astype(jnp.float32) + up.astype(jnp.float32)


def body(pair_density, coulomb, partners):
    mine = lax.axis_index("trans")
    pw = lax.axis_index("pw")
    core = mine & 1
    half = (mine >> 1) & 1
    offsets = (partners[0] - mine) & 63
    count = len(WIDTHS)
    starts = [sum(WIDTHS[:i]) for i in range(count)]
    away = [lax.dynamic_slice_in_dim(pair_density, (1 - half) * WIDE + at, width, 1) for at, width in zip(starts, WIDTHS)]
    more = jnp.pad(offsets.astype(jnp.bfloat16)[None, :], ((0, 15), (0, WIDTHS[-1] - SLOTS)))
    away[-1] = jnp.concatenate([away[-1], more])
    keep = lax.dynamic_slice_in_dim(pair_density, half * WIDE, WIDE, 1)
    away[0], keep = together(away[0], keep)
    other = [send(piece, other_half) for piece in away]
    keep_next = send(keep, previous_column)
    keep_last = send(keep, up_one, 0)
    weights = lax.dynamic_slice_in_dim(coulomb, half * WIDE, WIDE, 0)[None, :]

    def weigh(piece, at):
        piece = piece[:TB].astype(jnp.float32)
        return (piece * weights[:, at : at + piece.shape[1]]).astype(jnp.bfloat16)

    weighted = [weigh(keep, 0)]
    other[0], keep_next, keep_last = together(other[0], keep_next, keep_last)
    keep_swap = send(keep, other_core)
    other_next, other_last, other_swap, next_swap, last_swap = [], [], [], [], []
    for i in range(count):
        follow = send(other[i], previous_column)
        last = send(other[i], two_columns_back, 1)
        other_swap.append(send(other[i], other_core))
        weighted.append(weigh(other[i], starts[i]))
        if i == 0:
            keep_last = send(keep_last, up_to_owner, 0)
            keep_next_swap = send(keep_next, other_core)
        else:
            next_swap.append(send(other_next[-1], other_core))
            last_swap.append(send(other_last[-1], to_core_1, 1))
        if i == count - 1:
            far = other[i][TB, :SLOTS].astype(jnp.int32)
            keep_last_swap = send(keep_last, to_core_1, 0)
            far, weighted[-1], follow = together(far, weighted[-1], follow)
        else:
            follow, weighted[-1], weighted[0], keep_last = together(follow, weighted[-1], weighted[0], keep_last)
            other[i + 1], follow, last = together(other[i + 1], follow, last)
        other_next.append(follow)
        other_last.append(last)
    next_swap.append(send(other_next[-1], other_core))
    last_swap.append(send(other_last[-1], to_core_1, 1))
    wanted = jnp.where(half == 0, jnp.stack([offsets, far]), jnp.stack([far, offsets]))
    number = 2 * jnp.arange(2, dtype=jnp.int32)[:, None] + core + wanted
    pair = number >> 1
    low = (number & 1) ^ core
    entry = jnp.where(pair < 4, 2 * (pair ^ half) + low, 8 + 2 * half + low)
    table = jnp.concatenate([entry.reshape(-1), jnp.stack([half, half * 4 + pw])]).astype(jnp.int32)
    groups = [weighted[:1], weighted[1:]]
    groups += [[keep], [keep_swap], other, other_swap, [keep_next], [keep_next_swap], other_next, next_swap]
    groups += [[keep_last], [keep_last_swap], other_last, last_swap]
    return ring(partial_tiles(table, groups))


def solution(mesh):
    placed = (P("trans", "pw"), P("pw"), P("trans", None))
    return jax.shard_map(
        body, mesh=mesh, in_specs=placed, out_specs=P("trans", None, "pw"), check_vma=False
    )
```

```python
import functools

import jax
import jax.numpy as jnp
from jax import lax
from jax.experimental import pallas as pl
from jax.experimental.pallas import tpu as pltpu
from jax.sharding import PartitionSpec as P

SLOTS = 4
TB = 512
WIDE = 1024
WIDTHS = (640, 384)
DEPTH = 4
AXES = ("trans", "pw")


def place(device):
    trans, pw = divmod(device, 4)
    return trans // 16, trans // 4 % 4, trans // 2 % 2 * 4 + pw, trans % 2


def device_at(x, y, z, core):
    z %= 8
    return (((x % 4 * 4 + y % 4) * 2 + z // 4) * 2 + core) * 4 + z % 4


def send(value, target, half=None):
    pairs = []
    for device in range(256):
        x, y, z, core = place(device)
        there = target(x, y, z, core)
        if there is not None and half in (None, z // 4):
            pairs.append((device, device_at(*there)))
    return lax.ppermute(value, AXES, pairs)


def other_half(x, y, z, core):
    return x, y, z + 4, core


def other_core(x, y, z, core):
    return x, y, z, 1 - core


def to_core_1(x, y, z, core):
    return (x, y, z, 1) if core == 0 else None


def previous_column(x, y, z, core):
    column = (x * 4 + y - 1) % 16
    return column // 4, column % 4, z, core


def two_columns_back(x, y, z, core):
    column = (x * 4 + y - 2) % 16
    return column // 4, column % 4, z, core


def up_one(x, y, z, core):
    return x, y + 1, z, core


def up_to_owner(x, y, z, core):
    return (x if y in (3, 0) else x - 1), y + 1, z, core


def tile_kernel(counts, table, *refs):
    total = sum(counts)
    blocks = refs[:total]
    out, weighted, held, weighted_sem, sems = refs[total:]
    groups = []
    at = 0
    for count in counts:
        groups.append(blocks[at : at + count])
        at += count

    def copies(group, target, sem):
        start = 0
        for ref in group:
            width = ref.shape[1]
            pltpu.make_async_copy(ref.at[pl.ds(0, TB)], target.at[:, pl.ds(start, width)], sem).start()
            start += width

    def whole(target, sem):
        pltpu.make_async_copy(target, target, sem).wait()

    def fetch(tile, slot):
        for index, group in enumerate(groups[2:]):

            @pl.when(table[tile] == index)
            def _():
                copies(group, held.at[slot], sems.at[slot])

    half = table[8]
    z = table[9]
    for which in range(2):

        @pl.when(half == which)
        def _():
            copies(groups[which], weighted.at[0], weighted_sem.at[0])

    fetch(0, 0)
    fetch(1, 1)
    for which in range(2):

        @pl.when(half == which)
        def _():
            copies(groups[1 - which], weighted.at[1], weighted_sem.at[1])

    def step(tile, carry):
        owner = tile // SLOTS
        place = tile % SLOTS
        slot = tile % DEPTH

        @pl.when(tile + 2 < 2 * SLOTS)
        def _():
            fetch(tile + 2, (tile + 2) % DEPTH)

        @pl.when(place == 0)
        def _():
            whole(weighted.at[owner], weighted_sem.at[owner])

        whole(held.at[slot], sems.at[slot])
        result = lax.dot_general(
            weighted[owner], held[slot], (((1,), (1,)), ((), ())), preferred_element_type=jnp.float32
        )
        for part in range(4):
            column = result[:, part * 128 : (part + 1) * 128]
            ahead = (owner * 4 + part - z + 8) % 8

            out[ahead, place] = column.astype(jnp.bfloat16)

        return carry

    lax.fori_loop(0, 2 * SLOTS, step, 0)


def partial_tiles(table, groups):
    counts = [len(group) for group in groups]
    blocks = [piece for group in groups for piece in group]
    return pl.pallas_call(
        functools.partial(tile_kernel, counts),
        out_shape=jax.ShapeDtypeStruct((8, SLOTS, TB, 128), jnp.bfloat16),
        in_specs=[pl.BlockSpec(memory_space=pltpu.SMEM)] + [pl.BlockSpec(memory_space=pltpu.HBM)] * len(blocks),
        out_specs=pl.BlockSpec(memory_space=pltpu.VMEM),
        scratch_shapes=[
            pltpu.VMEM((2, TB, WIDE), jnp.bfloat16),
            pltpu.VMEM((DEPTH, TB, WIDE), jnp.bfloat16),
            pltpu.SemaphoreType.DMA((2,)),
            pltpu.SemaphoreType.DMA((DEPTH,)),
        ],
        compiler_params=pltpu.CompilerParams(vmem_limit_bytes=60 * 1024 * 1024),
        cost_estimate=pl.CostEstimate(flops=8 * 2 * TB * TB * WIDE, bytes_accessed=15 << 20, transcendentals=0),
    )(table, *blocks)


def together(*values):
    return lax.optimization_barrier(values)


def ring(parts):
    def ahead(x, y, z, core):
        return x, y, z + 1, core

    def behind(x, y, z, core):
        return x, y, z - 1, core

    down, up = together(send(parts[4, :2], behind), send(parts[4, 2:], ahead))
    for distance in range(3, 0, -1):
        lower, upper = parts[8 - distance].astype(jnp.float32), parts[distance].astype(jnp.float32)
        if distance == 3:
            down = jnp.concatenate([down, jnp.zeros_like(down)])
            up = jnp.concatenate([jnp.zeros_like(up), up])
        down = (lower + down.astype(jnp.float32)).astype(jnp.bfloat16)
        up = (upper + up.astype(jnp.float32)).astype(jnp.bfloat16)
        down, up = together(down, up)
        down, up = together(send(down, behind), send(up, ahead))
    return parts[0].astype(jnp.float32) + down.astype(jnp.float32) + up.astype(jnp.float32)


def body(pair_density, coulomb, partners):
    mine = lax.axis_index("trans")
    pw = lax.axis_index("pw")
    core = mine & 1
    half = (mine >> 1) & 1
    offsets = (partners[0] - mine) & 63
    count = len(WIDTHS)
    starts = [sum(WIDTHS[:i]) for i in range(count)]
    away = [lax.dynamic_slice_in_dim(pair_density, (1 - half) * WIDE + at, width, 1) for at, width in zip(starts, WIDTHS)]
    more = jnp.pad(offsets.astype(jnp.bfloat16)[None, :], ((0, 15), (0, WIDTHS[-1] - SLOTS)))
    away[-1] = jnp.concatenate([away[-1], more])
    keep = lax.dynamic_slice_in_dim(pair_density, half * WIDE, WIDE, 1)
    away[0], keep = together(away[0], keep)
    other = [send(away[0], other_half)]
    keep_next = send(keep, previous_column)
    keep_last = send(keep, up_one, 0)
    weights = lax.dynamic_slice_in_dim(coulomb, half * WIDE, WIDE, 0)[None, :]

    def weigh(piece, at):
        piece = piece[:TB].astype(jnp.float32)
        return (piece * weights[:, at : at + piece.shape[1]]).astype(jnp.bfloat16)

    weighted = [weigh(keep, 0)]
    other[0], keep_next, keep_last, away[1] = together(other[0], keep_next, keep_last, away[1])
    other.append(send(away[1], other_half))
    keep_swap = send(keep, other_core)
    other_next, other_last, other_swap, next_swap, last_swap = [], [], [], [], []
    for i in range(count):
        follow = send(other[i], previous_column)
        last = send(other[i], two_columns_back if i == count - 1 else up_one, 1)
        if i == count - 1:
            other_last[-1] = send(other_last[-1], up_to_owner, 1)
        other_swap.append(send(other[i], other_core))
        weighted.append(weigh(other[i], starts[i]))
        if i == 0:
            keep_last = send(keep_last, up_to_owner, 0)
            keep_next_swap = send(keep_next, other_core)
        else:
            next_swap.append(send(other_next[-1], other_core))
            last_swap.append(send(other_last[-1], to_core_1, 1))
        if i == count - 1:
            far = other[i][TB, :SLOTS].astype(jnp.int32)
            keep_last_swap = send(keep_last, to_core_1, 0)
            far, weighted[-1], follow = together(far, weighted[-1], follow)
        else:
            done = (follow, weighted[-1], weighted[0], keep_last, keep_swap, keep_next_swap, other_swap[-1])
            follow, weighted[-1], weighted[0], keep_last, keep_swap, keep_next_swap, other_swap[-1] = together(*done)
            other[i + 1], follow, last = together(other[i + 1], follow, last)
        other_next.append(follow)
        other_last.append(last)
    next_swap.append(send(other_next[-1], other_core))
    last_swap.append(send(other_last[-1], to_core_1, 1))
    wanted = jnp.where(half == 0, jnp.stack([offsets, far]), jnp.stack([far, offsets]))
    number = 2 * jnp.arange(2, dtype=jnp.int32)[:, None] + core + wanted
    pair = number >> 1
    low = (number & 1) ^ core
    entry = jnp.where(pair < 4, 2 * (pair ^ half) + low, 8 + 2 * half + low)
    table = jnp.concatenate([entry.reshape(-1), jnp.stack([half, half * 4 + pw])]).astype(jnp.int32)
    groups = [weighted[:1], weighted[1:]]
    groups += [[keep], [keep_swap], other, other_swap, [keep_next], [keep_next_swap], other_next, next_swap]
    groups += [[keep_last], [keep_last_swap], other_last, last_swap]
    return ring(partial_tiles(table, groups))


def solution(mesh):
    placed = (P("trans", "pw"), P("pw"), P("trans", None))
    return jax.shard_map(
        body, mesh=mesh, in_specs=placed, out_specs=P("trans", None, "pw"), check_vma=False
    )
```

```python
import functools

import jax
import jax.numpy as jnp
from jax import lax
from jax.experimental import pallas as pl
from jax.experimental.pallas import tpu as pltpu
from jax.sharding import PartitionSpec as P

SLOTS = 4
TB = 512
WIDE = 1024
WIDTHS = (512, 512)
DEPTH = 4
AXES = ("trans", "pw")


def place(device):
    trans, pw = divmod(device, 4)
    return trans // 16, trans // 4 % 4, trans // 2 % 2 * 4 + pw, trans % 2


def device_at(x, y, z, core):
    z %= 8
    return (((x % 4 * 4 + y % 4) * 2 + z // 4) * 2 + core) * 4 + z % 4


def send(value, target, half=None):
    pairs = []
    for device in range(256):
        x, y, z, core = place(device)
        there = target(x, y, z, core)
        if there is not None and half in (None, z // 4):
            pairs.append((device, device_at(*there)))
    return lax.ppermute(value, AXES, pairs)


def other_half(x, y, z, core):
    return x, y, z + 4, core


def other_core(x, y, z, core):
    return x, y, z, 1 - core


def to_core_1(x, y, z, core):
    return (x, y, z, 1) if core == 0 else None


def previous_column(x, y, z, core):
    column = (x * 4 + y - 1) % 16
    return column // 4, column % 4, z, core


def two_columns_back(x, y, z, core):
    column = (x * 4 + y - 2) % 16
    return column // 4, column % 4, z, core


def up_one(x, y, z, core):
    return x, y + 1, z, core


def up_to_owner(x, y, z, core):
    return (x if y in (3, 0) else x - 1), y + 1, z, core


def tile_kernel(counts, table, *refs):
    total = sum(counts)
    blocks = refs[:total]
    out, weighted, held, weighted_sem, sems = refs[total:]
    groups = []
    at = 0
    for count in counts:
        groups.append(blocks[at : at + count])
        at += count

    def copies(group, target, sem):
        start = 0
        for ref in group:
            width = ref.shape[1]
            pltpu.make_async_copy(ref.at[pl.ds(0, TB)], target.at[:, pl.ds(start, width)], sem).start()
            start += width

    def whole(target, sem):
        pltpu.make_async_copy(target, target, sem).wait()

    def fetch(tile, slot):
        for index, group in enumerate(groups[2:]):

            @pl.when(table[tile] == index)
            def _():
                copies(group, held.at[slot], sems.at[slot])

    half = table[8]
    z = table[9]
    for which in range(2):

        @pl.when(half == which)
        def _():
            copies(groups[which], weighted.at[0], weighted_sem.at[0])

    fetch(0, 0)
    fetch(1, 1)
    for which in range(2):

        @pl.when(half == which)
        def _():
            copies(groups[1 - which], weighted.at[1], weighted_sem.at[1])

    def step(tile, carry):
        owner = tile // SLOTS
        place = tile % SLOTS
        slot = tile % DEPTH

        @pl.when(tile + 2 < 2 * SLOTS)
        def _():
            fetch(tile + 2, (tile + 2) % DEPTH)

        @pl.when(place == 0)
        def _():
            whole(weighted.at[owner], weighted_sem.at[owner])

        whole(held.at[slot], sems.at[slot])
        result = lax.dot_general(
            weighted[owner], held[slot], (((1,), (1,)), ((), ())), preferred_element_type=jnp.float32
        )
        for part in range(4):
            column = result[:, part * 128 : (part + 1) * 128]
            ahead = (owner * 4 + part - z + 8) % 8

            out[ahead, place] = column.astype(jnp.bfloat16)

        return carry

    lax.fori_loop(0, 2 * SLOTS, step, 0)


def partial_tiles(table, groups):
    counts = [len(group) for group in groups]
    blocks = [piece for group in groups for piece in group]
    return pl.pallas_call(
        functools.partial(tile_kernel, counts),
        out_shape=jax.ShapeDtypeStruct((8, SLOTS, TB, 128), jnp.bfloat16),
        in_specs=[pl.BlockSpec(memory_space=pltpu.SMEM)] + [pl.BlockSpec(memory_space=pltpu.HBM)] * len(blocks),
        out_specs=pl.BlockSpec(memory_space=pltpu.VMEM),
        scratch_shapes=[
            pltpu.VMEM((2, TB, WIDE), jnp.bfloat16),
            pltpu.VMEM((DEPTH, TB, WIDE), jnp.bfloat16),
            pltpu.SemaphoreType.DMA((2,)),
            pltpu.SemaphoreType.DMA((DEPTH,)),
        ],
        compiler_params=pltpu.CompilerParams(vmem_limit_bytes=60 * 1024 * 1024),
        cost_estimate=pl.CostEstimate(flops=8 * 2 * TB * TB * WIDE, bytes_accessed=15 << 20, transcendentals=0),
    )(table, *blocks)


def together(*values):
    return lax.optimization_barrier(values)


def ring(parts):
    def ahead(x, y, z, core):
        return x, y, z + 1, core

    def behind(x, y, z, core):
        return x, y, z - 1, core

    down, up = together(send(parts[4, :2], behind), send(parts[4, 2:], ahead))
    for distance in range(3, 0, -1):
        lower, upper = parts[8 - distance].astype(jnp.float32), parts[distance].astype(jnp.float32)
        if distance == 3:
            down = jnp.concatenate([down, jnp.zeros_like(down)])
            up = jnp.concatenate([jnp.zeros_like(up), up])
        down = (lower + down.astype(jnp.float32)).astype(jnp.bfloat16)
        up = (upper + up.astype(jnp.float32)).astype(jnp.bfloat16)
        down, up = together(down, up)
        down, up = together(send(down, behind), send(up, ahead))
    return parts[0].astype(jnp.float32) + down.astype(jnp.float32) + up.astype(jnp.float32)


def body(pair_density, coulomb, partners):
    mine = lax.axis_index("trans")
    pw = lax.axis_index("pw")
    core = mine & 1
    half = (mine >> 1) & 1
    offsets = (partners[0] - mine) & 63
    count = len(WIDTHS)
    starts = [sum(WIDTHS[:i]) for i in range(count)]
    away = [lax.dynamic_slice_in_dim(pair_density, (1 - half) * WIDE + at, width, 1) for at, width in zip(starts, WIDTHS)]
    more = jnp.pad(offsets.astype(jnp.bfloat16)[None, :], ((0, 15), (0, WIDTHS[-1] - SLOTS)))
    away[-1] = jnp.concatenate([away[-1], more])
    keep = lax.dynamic_slice_in_dim(pair_density, half * WIDE, WIDE, 1)
    away[0], keep = together(away[0], keep)
    other = [send(away[0], other_half)]
    keep_next = send(keep, previous_column)
    keep_last = send(keep, up_one, 0)
    weights = lax.dynamic_slice_in_dim(coulomb, half * WIDE, WIDE, 0)[None, :]

    def weigh(piece, at):
        piece = piece[:TB].astype(jnp.float32)
        return (piece * weights[:, at : at + piece.shape[1]]).astype(jnp.bfloat16)

    weighted = [weigh(keep, 0)]
    other[0], keep_next, keep_last, away[1] = together(other[0], keep_next, keep_last, away[1])
    other.append(send(away[1], other_half))
    keep_swap = send(keep, other_core)
    other_next, other_last, other_swap, next_swap, last_swap = [], [], [], [], []
    for i in range(count):
        follow = send(other[i], previous_column)
        last = send(other[i], two_columns_back if i == count - 1 else up_one, 1)
        if i == count - 1:
            other_last[-1] = send(other_last[-1], up_to_owner, 1)
        other_swap.append(send(other[i], other_core))
        weighted.append(weigh(other[i], starts[i]))
        if i == 0:
            keep_last = send(keep_last, up_to_owner, 0)
            keep_next_swap = send(keep_next, other_core)
        else:
            next_swap.append(send(other_next[-1], other_core))
            last_swap.append(send(other_last[-1], to_core_1, 1))
        if i == count - 1:
            far = other[i][TB, :SLOTS].astype(jnp.int32)
            keep_last_swap = send(keep_last, to_core_1, 0)
            far, weighted[-1], follow = together(far, weighted[-1], follow)
        else:
            done = (follow, weighted[-1], weighted[0], keep_last, keep_swap, keep_next_swap, other_swap[-1])
            follow, weighted[-1], weighted[0], keep_last, keep_swap, keep_next_swap, other_swap[-1] = together(*done)
            other[i + 1], follow, last = together(other[i + 1], follow, last)
        other_next.append(follow)
        other_last.append(last)
    next_swap.append(send(other_next[-1], other_core))
    last_swap.append(send(other_last[-1], to_core_1, 1))
    wanted = jnp.where(half == 0, jnp.stack([offsets, far]), jnp.stack([far, offsets]))
    number = 2 * jnp.arange(2, dtype=jnp.int32)[:, None] + core + wanted
    pair = number >> 1
    low = (number & 1) ^ core
    entry = jnp.where(pair < 4, 2 * (pair ^ half) + low, 8 + 2 * half + low)
    table = jnp.concatenate([entry.reshape(-1), jnp.stack([half, half * 4 + pw])]).astype(jnp.int32)
    groups = [weighted[:1], weighted[1:]]
    groups += [[keep], [keep_swap], other, other_swap, [keep_next], [keep_next_swap], other_next, next_swap]
    groups += [[keep_last], [keep_last_swap], other_last, last_swap]
    return ring(partial_tiles(table, groups))


def solution(mesh):
    placed = (P("trans", "pw"), P("pw"), P("trans", None))
    return jax.shard_map(
        body, mesh=mesh, in_specs=placed, out_specs=P("trans", None, "pw"), check_vma=False
    )
```
